1024 devices in a mesh: dp: 256 (over y, z, core), table: 4 (over x).
Axes of the slice: x: 4, y: 4, z: 32, core: 2. Of those that a mesh axis runs over, the one named last changes fastest.
Arguments:
- embeddings: bfloat16 [1024, 192, 512], P(('dp', 'table')), may hold values from -6 to 6
- lengths: int32 [1024], P(('dp', 'table')), may hold values from 16 to 192, as said below
- cotangent: bfloat16 [1024, 192, 512], P(('dp', 'table')), may hold values from -6 to 6
- w_proj: bfloat16 [512, 2048], replicated, may hold values from -0.25 to 0.25
- w_out: bfloat16 [512, 512], replicated, may hold values from -0.25 to 0.25
- routes: int32 [1024, 192, 1], P(('dp', 'table')), may hold values from 0 to 4; in each aligned block of 192 rows (0 to 191, 192 to 383, ..., all dimensions but the last counted through in order) at most 64 rows name the same one
- hot_ids: int32 [1024, 192], P(('dp', 'table')), may hold values from 0 to 1023
- cold_ids: int32 [1024, 192], P(('dp', 'table')), may hold values from 0 to 127
Outputs:
- hot_grad: float32 [1024, 512], P('dp')
- cold_grad: float32 [131072, 512], P(('dp', 'table'))
The draws below stay inside these ranges and needn't reach their ends.
Inputs may be any that keep to these rules, and one draw needn't show every extreme that they name: `lengths`: every history has at least 16 valid items, and some history has 192. `routes`: among the 192 positions of one device, each of the values 0 to 4 appears at most 64 times.
All inputs are finite; a program needn't handle non-finite values.
Results may differ from the reference program's by a relative error of at most 0.015.
Values may be sent and summed in bfloat16 or wider, within the bound.
No kernel may reach another device: no remote copies, remote signals or barrier semaphores. Data moves between devices by JAX's collectives and lax.ppermute only.
A program may use at most 32 MiB of HBM per device.

```python
import math
import jax
import jax.numpy as jnp
import numpy as np
from jax import lax

D = 512
HEAD_DIM = 64
SEQ_LEN = 192
COLD_DEV = 128
ROWS_DEV = 192
CAP = 64
SEQS = 1024
HOT = 1024
COLD = 131072
N_TABLE = 4


def draw_lengths(key, part):
    key = jax.random.fold_in(key, 11)
    key_draw, key_pick = jax.random.split(key)
    drawn = jax.random.randint(key_draw, (SEQS,), 16, SEQ_LEN + 1)
    chosen = jax.random.randint(key_pick, (), 0, SEQS)
    return jnp.where(jnp.arange(SEQS) == chosen, SEQ_LEN, drawn).astype(jnp.int32)


def touch_ends(values, stream_key, least, top_value):
    spot = [jax.random.randint(jax.random.fold_in(stream_key, axis), (), 0, length) for axis, length in enumerate(values.shape)]
    longest = values.shape.index(max(values.shape))
    beside = spot[:longest] + [(spot[longest] + 1) % values.shape[longest]] + spot[longest + 1:]
    return values.at[tuple(spot)].set(least).at[tuple(beside)].set(top_value)


def shard_levels(own_key, dims, cuts, smallest, top_value):
    def one(dim, parts):
        heights = jax.random.uniform(jax.random.fold_in(jax.random.fold_in(own_key, 6), dim), (parts,), jnp.float32, smallest / len(cuts), top_value / len(cuts))
        return jnp.repeat(jnp.exp(heights), dims[dim] // parts).reshape((-1,) + (1,) * (len(dims) - dim - 1))

    loudness = one(*cuts[0])
    for cut in cuts[1:]:
        loudness = loudness * one(*cut)
    return loudness


def rank_bounds(number_of, lean):
    portions = [(1 << 20) // math.isqrt(grade ** lean) + 1 for grade in range(1, number_of + 1)]
    spread = 1 + sum(portions) // (1 << 30)
    return np.cumsum(np.array([max(1, weight // spread) for weight in portions]))


def skewed_ids(own_key, dims, amount, skew):
    table = rank_bounds(amount, skew)
    ticket = jax.random.randint(jax.random.fold_in(own_key, 1), dims, 0, int(table[amount - 1]))
    rank = jnp.searchsorted(jnp.asarray(table, jnp.int32), ticket, side="right")
    return jax.random.permutation(jax.random.fold_in(own_key, 2), amount)[rank].astype(jnp.int32)


def assign_block(own_key, own, number, rows, amount, top, limit, slope):
    order = jax.random.permutation(own_key, amount)
    crowded, ordinary = shares(amount, rows * top, limit, slope, True), shares(amount, rows * top, limit, slope, False)
    places = jnp.arange(amount)

    def named(sizes, rotation):
        used = int((sizes > 0).sum())
        fixed = max(1, used // 4)
        moved = fixed + (places - fixed + rotation * (used - fixed)) % max(1, amount - fixed)
        return jnp.zeros((amount,), jnp.int32).at[order[jnp.where(places < fixed, places, moved)]].set(jnp.asarray(sizes, jnp.int32))

    sizes = jnp.where(number % 4 == 0, named(crowded, number // 4), named(ordinary, number - number // 4 - 1))
    mixed = jax.random.permutation(jax.random.fold_in(own, 3), amount)
    source_of, taker = mixed[0:amount // 2 * 2:2], mixed[1:amount // 2 * 2:2]
    margin = jnp.minimum(sizes[source_of] - 1, limit - sizes[taker]) // 2
    margin = jnp.where((source_of == order[0]) | (taker == order[0]) | (sizes[taker] == 0), 0, jnp.maximum(margin, 0))
    moved = jax.random.randint(jax.random.fold_in(own, 4), (amount // 2,), 0, 1 << 20) % (margin + 1)
    sizes = sizes.at[source_of].add(-moved).at[taker].add(moved)
    labels = jnp.searchsorted(jnp.cumsum(sizes), jnp.arange(rows * top), side="right").astype(jnp.int32)
    grid = labels.reshape(top, rows).T
    grid = grid[jax.random.permutation(jax.random.fold_in(own, 1), rows)]
    rotation = jax.random.randint(jax.random.fold_in(own, 2), (rows, 1), 0, top)
    return jnp.take_along_axis(grid, (jnp.arange(top)[None, :] + rotation) % top, axis=1)


def shares(number_of, total, bound, slope, full):
    weights = [(1 << 20) // math.isqrt(rank ** slope) + 1 for rank in range(1, number_of + 1)]
    largest = bound if full else min(bound, max(-(-total // number_of), total * weights[0] // sum(weights)))
    least = 1 if total - largest >= number_of - 1 else 0
    holding, spare = [largest] + [least] * (number_of - 1), total - largest - least * (number_of - 1)
    while spare > 0:
        candidates = [i for i in range(1, number_of) if holding[i] < largest] or [i for i in range(1, number_of) if holding[i] < bound]
        whole, remaining = sum([weights[i] for i in candidates]), spare
        for i in candidates:
            extra = min(bound - holding[i], max(1, remaining * weights[i] // whole), spare)
            holding[i] = holding[i] + extra
            spare = spare - extra
    return np.array(holding)


def normal_values(rng, shape, spread, reach, shards=(), kind=jnp.bfloat16):
    values = spread * jax.random.normal(rng, shape, jnp.float32)
    if shards:
        values = values * shard_levels(rng, shape, shards, -0.22, 0.18)
    return jnp.clip(values, -reach, reach).astype(kind)


def setup_inputs(seed: int = 0) -> dict:
    key_of = jax.random.split(jax.random.key(seed), 9)
    embeddings = normal_values(key_of[0], (SEQS, SEQ_LEN, D), 1.0, 6.0, ((0, 1024),))
    lengths = draw_lengths(jax.random.fold_in(key_of[8], 71), 0)
    cotangent = normal_values(key_of[2], (SEQS, SEQ_LEN, D), 1.0, 6.0, ((0, 1024),))
    w_proj = normal_values(key_of[3], (D, 4 * D), D ** -0.5, 0.25)
    w_out = normal_values(key_of[4], (D, D), D ** -0.5, 0.25)
    routes_keys = jax.random.split(jax.random.fold_in(key_of[5], 1), SEQS * SEQ_LEN // ROWS_DEV)
    routes_turns = jax.random.permutation(jax.random.fold_in(key_of[5], 3), SEQS * SEQ_LEN // ROWS_DEV)
    routes = jax.vmap(lambda own, number: assign_block(jax.random.fold_in(key_of[5], 2), own, number, ROWS_DEV, N_TABLE + 1, 1, CAP, 2))(routes_keys, routes_turns).reshape((SEQS, SEQ_LEN, 1))
    hot_ids = touch_ends(skewed_ids(key_of[6], (SEQS, SEQ_LEN), HOT, 2), jax.random.fold_in(key_of[6], 3), 0, HOT - 1).astype(jnp.int32)
    cold_ids = touch_ends(jax.random.randint(key_of[7], (SEQS, SEQ_LEN), 0, COLD_DEV), jax.random.fold_in(key_of[7], 1), 0, COLD_DEV - 1).astype(jnp.int32)
    return {"embeddings": embeddings, "lengths": lengths, "cotangent": cotangent, "w_proj": w_proj, "w_out": w_out, "routes": routes, "hot_ids": hot_ids, "cold_ids": cold_ids}


epsilon = 1e-06

def layer_output(embedded, length, w_proj, w_out):
    seq_len = embedded.shape[0]
    model_width = embedded.shape[1]
    head_count = model_width // HEAD_DIM
    inputs = embedded.astype(jnp.float32)
    normed = (inputs * lax.rsqrt(lax.optimization_barrier(jnp.mean(inputs * inputs, axis=-1, keepdims=True)) + epsilon)).astype(jnp.bfloat16)
    projected = jax.nn.silu(jnp.dot(normed, w_proj, preferred_element_type=jnp.float32)).astype(jnp.bfloat16)
    gate_part, value_part, query_part, key_part = jnp.split(projected, 4, axis=1)
    head_shape = (seq_len, head_count, HEAD_DIM)
    queries = query_part.reshape(head_shape).astype(jnp.float32)
    keys_all = key_part.reshape(head_shape).astype(jnp.float32)
    values_all = value_part.reshape(head_shape).astype(jnp.float32)
    scores = jnp.einsum('ihd,jhd->hij', queries, keys_all) * HEAD_DIM ** (-0.5)
    position = jnp.arange(seq_len)
    visible = (position[None, :] <= position[:, None]) & (position[:, None] < length)
    weights = (jnp.where(visible[None], jax.nn.silu(scores), 0.0) / length.astype(jnp.float32)).astype(jnp.bfloat16)
    attended = jnp.einsum('hij,jhd->ihd', weights.astype(jnp.float32), values_all).reshape(seq_len, model_width)
    mixed = (attended * lax.rsqrt(lax.optimization_barrier(jnp.mean(attended * attended, axis=-1, keepdims=True)) + epsilon) * gate_part.astype(jnp.float32)).astype(jnp.bfloat16)
    return inputs + jnp.dot(mixed, w_out, preferred_element_type=jnp.float32)

def item_gradient(embedded, length, cotangent, w_proj, w_out):

    def forward(embedded_in):
        return layer_output(embedded_in, length, w_proj, w_out)
    output, backward = jax.vjp(forward, embedded)
    grad_rows, = backward(cotangent.astype(output.dtype))
    position = jnp.arange(embedded.shape[0])
    return jnp.where((position < length)[:, None], grad_rows, jnp.zeros_like(grad_rows))

def reference(embeddings, lengths, cotangent, w_proj, w_out, routes, hot_ids, cold_ids):

    def per_sequence(packed):
        return item_gradient(packed[0], packed[1], packed[2], w_proj, w_out)
    item_grad = lax.map(per_sequence, (embeddings, lengths, cotangent))
    row_total = item_grad.shape[0] * item_grad.shape[1]
    flat_grad = item_grad.reshape(row_total, item_grad.shape[2]).astype(jnp.float32)
    route_flat = routes.reshape(row_total)
    hot_flat = hot_ids.reshape(row_total)
    cold_flat = cold_ids.reshape(row_total)
    is_hot = route_flat == N_TABLE
    hot_grad = jax.ops.segment_sum(jnp.where(is_hot[:, None], flat_grad, 0.0), hot_flat, num_segments=HOT)
    group = jnp.arange(row_total) // ROWS_DEV // N_TABLE
    target = jnp.where(is_hot, 0, (group * N_TABLE + route_flat) * COLD_DEV + cold_flat).astype(jnp.int32)
    cold_grad = jax.ops.segment_sum(jnp.where(is_hot[:, None], 0.0, flat_grad), target, num_segments=COLD)
    return (hot_grad, cold_grad)
```

```python
import functools

import jax
import jax.numpy as jnp
from jax import lax
from jax.experimental import pallas as pl
from jax.experimental.pallas import tpu as pltpu
from jax.sharding import Mesh
from jax.sharding import PartitionSpec as P

HEAD_DIM = 64
HOT_DEV = 4
COLD_DEV = 128
CAP = 64
ID_ROWS = 16
ID_BASE = 32
PAIR = 2 * HEAD_DIM

epsilon = 1e-06
bf16 = jnp.bfloat16
f32 = jnp.float32


def dot(a, b, contract=((1,), (0,))):
    return lax.dot_general(a, b, (contract, ((), ())), preferred_element_type=f32)


def sigmoid(v):
    return 0.5 * jnp.tanh(0.5 * v) + 0.5


def item_kernel(owners, length_ref, emb_ref, cot_ref, w_proj_ref, w_out_ref, routes_ref, hot_ref, cold_ref, hot_out, cold_out, proj, slope, weight, factor, attended, heads_grad):
    seq, width = emb_ref.shape
    pairs = width // PAIR
    length = length_ref[0]

    x = emb_ref[...].astype(f32)
    root = lax.rsqrt(jnp.mean(x * x, axis=1, keepdims=True) + epsilon)
    xn = x * root
    normed = xn.astype(bf16)
    for part in range(4):
        cols = slice(part * width, (part + 1) * width)
        pre = dot(normed, w_proj_ref[:, cols])
        gate = sigmoid(pre)
        act = pre * gate
        slope[:, cols] = gate + act * (1.0 - gate)
        scale = HEAD_DIM ** (-0.5) if part == 2 else 1.0
        proj[:, cols] = (act.astype(bf16) * jnp.asarray(scale, bf16))

    rows = lax.broadcasted_iota(jnp.int32, (seq, seq), 0)
    lanes = lax.broadcasted_iota(jnp.int32, (seq, seq), 1)
    inverse = 1.0 / jnp.full((seq, seq), length, jnp.int32).astype(f32)
    mask = jnp.where((lanes <= rows) & (rows < length), inverse, 0.0)
    low = lax.broadcasted_iota(jnp.int32, (seq, PAIR), 1) < HEAD_DIM

    def split_heads(block):
        zero = jnp.zeros_like(block)
        return jnp.concatenate([jnp.where(low, block, zero), jnp.where(low, zero, block)], axis=0)

    def join_heads(block):
        return jnp.where(low, block[:seq], block[seq:])

    def part_of(part, pair):
        return proj[:, part * width + pair * PAIR : part * width + (pair + 1) * PAIR]

    for pair in range(pairs):
        scores = dot(split_heads(part_of(2, pair)), part_of(3, pair), ((1,), (1,)))
        for head in range(2):
            score = scores[head * seq : (head + 1) * seq]
            gate = sigmoid(score)
            act = score * gate
            weight[pair, head * seq : (head + 1) * seq, :] = (act * mask).astype(bf16)
            factor[pair, head * seq : (head + 1) * seq, :] = (gate + act * (1.0 - gate)) * mask
        attended[:, pair * PAIR : (pair + 1) * PAIR] = join_heads(dot(weight[pair], part_of(1, pair)))

    att = attended[...]
    att_root = lax.rsqrt(jnp.mean(att * att, axis=1, keepdims=True) + epsilon)
    att_n = att * att_root
    mixed_grad = dot(cot_ref[...], w_out_ref[...], ((1,), (1,))).astype(bf16).astype(f32)
    gate_part = proj[:, :width].astype(f32)
    gate_grad = (mixed_grad * att_n).astype(bf16).astype(f32)
    proj[:, :width] = (gate_grad * slope[:, :width]).astype(bf16)
    att_n_grad = mixed_grad * gate_part
    inner = jnp.mean(att_n_grad * att_n, axis=1, keepdims=True)
    heads_grad[...] = (att_root * (att_n_grad - att_n * inner)).astype(bf16)

    for pair in range(pairs):
        query, key, value = part_of(2, pair), part_of(3, pair), part_of(1, pair)
        grad_split = split_heads(heads_grad[:, pair * PAIR : (pair + 1) * PAIR])
        weight_grad = dot(grad_split, value, ((1,), (1,))).astype(bf16).astype(f32)
        score_grad = (weight_grad * factor[pair]).astype(bf16)
        value_grad = dot(weight[pair], grad_split, ((0,), (0,)))
        query_grad = join_heads(dot(score_grad, key)) * HEAD_DIM ** (-0.5)
        key_grad = dot(score_grad, split_heads(query), ((0,), (0,)))
        for part, grad in ((1, value_grad), (2, query_grad), (3, key_grad)):
            cols = slice(part * width + pair * PAIR, part * width + (pair + 1) * PAIR)
            proj[:, cols] = (grad.astype(bf16).astype(f32) * slope[:, cols]).astype(bf16)

    normed_grad = dot(proj[...], w_proj_ref[...], ((1,), (1,))).astype(bf16).astype(f32)
    inner = jnp.mean(normed_grad * xn, axis=1, keepdims=True)
    total = root * (normed_grad - xn * inner) + cot_ref[...].astype(f32)
    valid = lax.broadcasted_iota(jnp.int32, (seq, width), 0) < length
    grad_rows = jnp.where(valid, total, 0.0).astype(bf16)

    route = routes_ref[...]
    hot_id = hot_ref[...]
    is_hot = route == owners
    target = jnp.where(is_hot, -1, route * COLD_DEV + cold_ref[...])
    for owner in range(owners):
        bucket = lax.broadcasted_iota(jnp.int32, (COLD_DEV, seq), 0) + owner * COLD_DEV
        chosen = jnp.where(bucket == target, 1.0, 0.0).astype(bf16)
        cold_out[owner * COLD_DEV : (owner + 1) * COLD_DEV, :] = dot(chosen, grad_rows)

    before = jnp.where(rows < lanes, 1.0, 0.0).astype(bf16)
    hot_flag = jnp.where(is_hot, 1.0, 0.0)
    place = dot(hot_flag.astype(bf16), before).astype(jnp.int32)
    place = jnp.where(is_hot, place, -1)
    slots = lax.broadcasted_iota(jnp.int32, (CAP, seq), 0)
    chosen = jnp.where(slots == place, 1.0, 0.0).astype(bf16)
    hot_out[:CAP, :] = dot(chosen, grad_rows).astype(bf16)
    high = lax.shift_right_logical(hot_id, 5).astype(f32)
    rest = (hot_id & (ID_BASE - 1)).astype(f32)
    which = lax.broadcasted_iota(jnp.int32, (ID_ROWS, seq), 0)
    ids = jnp.where(which == 0, high, jnp.where(which == 1, rest, jnp.where(which == 2, 1.0, 0.0))).astype(bf16)
    slot_ids = dot(ids, chosen, ((1,), (1,)))
    hot_out[CAP:, :] = jnp.zeros((ID_ROWS, width), bf16)
    hot_out[CAP:, :PAIR] = jnp.concatenate([slot_ids, jnp.zeros((ID_ROWS, PAIR - CAP), f32)], axis=1).astype(bf16)


def item_call(owners, length, emb, cot, w_proj, w_out, routes, hot_ids, cold_ids):
    seq, width = emb.shape
    pairs = width // PAIR
    whole = pl.BlockSpec(memory_space=pltpu.VMEM)
    return pl.pallas_call(
        functools.partial(item_kernel, owners),
        in_specs=[pl.BlockSpec(memory_space=pltpu.SMEM)] + [whole] * 7,
        out_specs=[whole, whole],
        out_shape=[
            jax.ShapeDtypeStruct((CAP + ID_ROWS, width), bf16),
            jax.ShapeDtypeStruct((owners * COLD_DEV, width), f32),
        ],
        scratch_shapes=[
            pltpu.VMEM((seq, 4 * width), bf16),
            pltpu.VMEM((seq, 4 * width), f32),
            pltpu.VMEM((pairs, 2 * seq, seq), bf16),
            pltpu.VMEM((pairs, 2 * seq, seq), f32),
            pltpu.VMEM((seq, width), f32),
            pltpu.VMEM((seq, width), bf16),
        ],
        compiler_params=pltpu.CompilerParams(vmem_limit_bytes=48 * 1024 * 1024),
        cost_estimate=pl.CostEstimate(flops=1_200_000_000, bytes_accessed=4_500_000, transcendentals=700_000),
        name="item_grad",
    )(length, emb, cot, w_proj, w_out, routes, hot_ids, cold_ids)


def hot_kernel(z_size, cores, base_ref, rows_ref, out_ref):
    members = rows_ref.shape[0] // (CAP + ID_ROWS)
    buckets = z_size * HOT_DEV
    place = lax.broadcasted_iota(jnp.int32, (buckets, CAP), 0)
    bucket = (place // HOT_DEV) * (HOT_DEV * cores) + place % HOT_DEV + base_ref[0]
    total = jnp.zeros((buckets, rows_ref.shape[1]), f32)
    for member in range(members):
        start = member * (CAP + ID_ROWS)
        ids = rows_ref[start + CAP : start + CAP + ID_ROWS, :CAP].astype(f32)
        slot_id = ids[0:1] * ID_BASE + ids[1:2]
        slot_id = jnp.where(ids[2:3] > 0.5, slot_id, -1.0).astype(jnp.int32)
        chosen = jnp.where(bucket == slot_id, 1.0, 0.0).astype(bf16)
        total = total + dot(chosen, rows_ref[start : start + CAP, :])
    out_ref[...] = total.astype(bf16)


def hot_call(z_size, cores, base, rows):
    whole = pl.BlockSpec(memory_space=pltpu.VMEM)
    return pl.pallas_call(
        functools.partial(hot_kernel, z_size, cores),
        in_specs=[pl.BlockSpec(memory_space=pltpu.SMEM), whole],
        out_specs=whole,
        out_shape=jax.ShapeDtypeStruct((z_size * HOT_DEV, rows.shape[1]), bf16),
        cost_estimate=pl.CostEstimate(flops=80_000_000, bytes_accessed=800_000, transcendentals=0),
        name="hot_sum",
    )(base, rows)


def shards(embeddings, lengths, cotangent, w_proj, w_out, routes, hot_ids, cold_ids):
    owners = lax.axis_size("table")
    z_size, cores = lax.axis_size("z"), lax.axis_size("core")
    seq, width = embeddings.shape[1:]
    hot_rows, dense_cold = item_call(
        owners, lengths, embeddings.reshape(seq, width), cotangent.reshape(seq, width), w_proj, w_out,
        routes.reshape(1, seq), hot_ids, cold_ids,
    )
    cold_grad = lax.psum_scatter(dense_cold, "table", scatter_dimension=0, tiled=True)
    gathered = lax.all_gather(hot_rows, ("y", "core"), tiled=True)
    base = lax.axis_index("y") * (z_size * cores * HOT_DEV) + lax.axis_index("core") * HOT_DEV
    partial = hot_call(z_size, cores, base.reshape(1).astype(jnp.int32), gathered)
    parts = lax.all_to_all(partial.reshape(z_size, HOT_DEV, width), "z", 0, 0)
    share = jnp.sum(parts.astype(f32), axis=0)
    hot_grad = lax.psum(share, "table")
    return (hot_grad, cold_grad)


def solution(mesh):
    dp, table = mesh.devices.shape
    cores, y_size = 2, 4
    fine = Mesh(mesh.devices.reshape(y_size, dp // (y_size * cores), cores, table), ("y", "z", "core", "table"))
    every = ("y", "z", "core", "table")
    return jax.shard_map(
        shards,
        mesh=fine,
        in_specs=(
            P(every, None, None),
            P(every),
            P(every, None, None),
            P(),
            P(),
            P(every, None, None),
            P(every, None),
            P(every, None),
        ),
        out_specs=(P(("y", "z", "core"), None), P(every, None)),
        check_vma=False,
    )
```

```python
import functools

import jax
import jax.numpy as jnp
from jax import lax
from jax.experimental import pallas as pl
from jax.experimental.pallas import tpu as pltpu
from jax.sharding import Mesh
from jax.sharding import PartitionSpec as P

HEAD_DIM = 64
HOT_DEV = 4
COLD_DEV = 128
CAP = 64
ID_ROWS = 16
ID_BASE = 32
PAIR = 2 * HEAD_DIM

epsilon = 1e-06
bf16 = jnp.bfloat16
f32 = jnp.float32


def dot(a, b, contract=((1,), (0,))):
    return lax.dot_general(a, b, (contract, ((), ())), preferred_element_type=f32)


def sigmoid(v):
    return 0.5 * jnp.tanh(0.5 * v) + 0.5


def item_kernel(owners, *refs):
    length_ref, emb_hbm, cot_hbm, w_proj_hbm, w_out_hbm, routes_hbm, hot_hbm, cold_hbm = refs[:8]
    hot_out, cold_out = refs[8:10]
    emb_ref, cot_ref, w_proj_ref, w_out_ref, routes_ref, hot_ref, cold_ref = refs[10:17]
    proj, slope, weight, factor, attended, heads_grad, sems = refs[17:]
    seq, width = emb_ref.shape
    pairs = width // PAIR
    length = length_ref[0]

    loads = [(emb_hbm, emb_ref)]
    for part in (2, 3, 1, 0):
        cols = pl.ds(part * width, width)
        loads.append((w_proj_hbm.at[:, cols], w_proj_ref.at[:, cols]))
    loads += [(cot_hbm, cot_ref), (w_out_hbm, w_out_ref), (routes_hbm, routes_ref), (hot_hbm, hot_ref), (cold_hbm, cold_ref)]
    loads = [pltpu.make_async_copy(src, dst, sems.at[i]) for i, (src, dst) in enumerate(loads)]
    for load in loads:
        load.start()

    loads[0].wait()
    x = emb_ref[...].astype(f32)
    root = lax.rsqrt(jnp.mean(x * x, axis=1, keepdims=True) + epsilon)
    xn = x * root
    normed = xn.astype(bf16)
    for step, part in enumerate((2, 3, 1, 0)):
        cols = slice(part * width, (part + 1) * width)
        loads[1 + step].wait()
        pre = dot(normed, w_proj_ref[:, cols])
        gate = sigmoid(pre)
        act = pre * gate
        slope[:, cols] = gate + act * (1.0 - gate)
        scale = HEAD_DIM ** (-0.5) if part == 2 else 1.0
        proj[:, cols] = (act.astype(bf16) * jnp.asarray(scale, bf16))

    rows = lax.broadcasted_iota(jnp.int32, (seq, seq), 0)
    lanes = lax.broadcasted_iota(jnp.int32, (seq, seq), 1)
    inverse = 1.0 / jnp.full((seq, seq), length, jnp.int32).astype(f32)
    mask = jnp.where((lanes <= rows) & (rows < length), inverse, 0.0)
    low = lax.broadcasted_iota(jnp.int32, (seq, PAIR), 1) < HEAD_DIM

    def split_heads(block):
        zero = jnp.zeros_like(block)
        return jnp.concatenate([jnp.where(low, block, zero), jnp.where(low, zero, block)], axis=0)

    def join_heads(block):
        return jnp.where(low, block[:seq], block[seq:])

    def part_of(part, pair):
        return proj[:, part * width + pair * PAIR : part * width + (pair + 1) * PAIR]

    for pair in range(pairs):
        scores = dot(split_heads(part_of(2, pair)), part_of(3, pair), ((1,), (1,)))
        for head in range(2):
            score = scores[head * seq : (head + 1) * seq]
            gate = sigmoid(score)
            act = score * gate
            weight[pair, head * seq : (head + 1) * seq, :] = (act * mask).astype(bf16)
            factor[pair, head * seq : (head + 1) * seq, :] = (gate + act * (1.0 - gate)) * mask
        attended[:, pair * PAIR : (pair + 1) * PAIR] = join_heads(dot(weight[pair], part_of(1, pair)))

    loads[5].wait()
    loads[6].wait()
    att = attended[...]
    att_root = lax.rsqrt(jnp.mean(att * att, axis=1, keepdims=True) + epsilon)
    att_n = att * att_root
    mixed_grad = dot(cot_ref[...], w_out_ref[...], ((1,), (1,))).astype(bf16).astype(f32)
    gate_part = proj[:, :width].astype(f32)
    gate_grad = (mixed_grad * att_n).astype(bf16).astype(f32)
    proj[:, :width] = (gate_grad * slope[:, :width]).astype(bf16)
    att_n_grad = mixed_grad * gate_part
    inner = jnp.mean(att_n_grad * att_n, axis=1, keepdims=True)
    heads_grad[...] = (att_root * (att_n_grad - att_n * inner)).astype(bf16)

    for pair in range(pairs):
        query, key, value = part_of(2, pair), part_of(3, pair), part_of(1, pair)
        grad_split = split_heads(heads_grad[:, pair * PAIR : (pair + 1) * PAIR])
        weight_grad = dot(grad_split, value, ((1,), (1,))).astype(bf16).astype(f32)
        score_grad = (weight_grad * factor[pair]).astype(bf16)
        value_grad = dot(weight[pair], grad_split, ((0,), (0,)))
        query_grad = join_heads(dot(score_grad, key)) * HEAD_DIM ** (-0.5)
        key_grad = dot(score_grad, split_heads(query), ((0,), (0,)))
        for part, grad in ((1, value_grad), (2, query_grad), (3, key_grad)):
            cols = slice(part * width + pair * PAIR, part * width + (pair + 1) * PAIR)
            proj[:, cols] = (grad.astype(bf16).astype(f32) * slope[:, cols]).astype(bf16)

    normed_grad = dot(proj[...], w_proj_ref[...], ((1,), (1,))).astype(bf16).astype(f32)
    inner = jnp.mean(normed_grad * xn, axis=1, keepdims=True)
    total = root * (normed_grad - xn * inner) + cot_ref[...].astype(f32)
    valid = lax.broadcasted_iota(jnp.int32, (seq, width), 0) < length
    grad_rows = jnp.where(valid, total, 0.0).astype(bf16)

    for load in loads[7:]:
        load.wait()
    route = routes_ref[...]
    bucket = jnp.where(route == owners, hot_ref[...], cold_ref[...])
    kind = lax.broadcasted_iota(jnp.int32, (ID_ROWS, seq), 0)
    named = kind == route
    before = jnp.where(rows < lanes, 1.0, 0.0).astype(bf16)
    place = dot(jnp.where(named, 1.0, 0.0).astype(bf16), before).astype(jnp.int32)
    place = jnp.where(named, place, -1)
    high = lax.shift_right_logical(bucket, 5).astype(f32)
    rest = (bucket & (ID_BASE - 1)).astype(f32)
    ids = jnp.where(kind == 0, high, jnp.where(kind == 1, rest, jnp.where(kind == 2, 1.0, 0.0))).astype(bf16)
    slots = lax.broadcasted_iota(jnp.int32, (CAP, seq), 0)
    for owner in range(owners + 1):
        out = hot_out if owner == owners else cold_out.at[owner]
        chosen = jnp.where(slots == place[owner : owner + 1], 1.0, 0.0).astype(bf16)
        out[:CAP, :] = dot(chosen, grad_rows).astype(bf16)
        slot_ids = dot(ids, chosen, ((1,), (1,)))
        out[CAP:, :] = jnp.zeros((ID_ROWS, width), bf16)
        out[CAP:, :PAIR] = jnp.concatenate([slot_ids, jnp.zeros((ID_ROWS, PAIR - CAP), f32)], axis=1).astype(bf16)


def item_call(owners, length, emb, cot, w_proj, w_out, routes, hot_ids, cold_ids):
    seq, width = emb.shape
    pairs = width // PAIR
    whole = pl.BlockSpec(memory_space=pltpu.VMEM)
    loaded = (emb, cot, w_proj, w_out, routes, hot_ids, cold_ids)
    return pl.pallas_call(
        functools.partial(item_kernel, owners),
        in_specs=[pl.BlockSpec(memory_space=pltpu.SMEM)] + [pl.BlockSpec(memory_space=pltpu.HBM)] * 7,
        out_specs=[whole, whole],
        out_shape=[
            jax.ShapeDtypeStruct((CAP + ID_ROWS, width), bf16),
            jax.ShapeDtypeStruct((owners, CAP + ID_ROWS, width), bf16),
        ],
        scratch_shapes=[pltpu.VMEM(a.shape, a.dtype) for a in loaded]
        + [
            pltpu.VMEM((seq, 4 * width), bf16),
            pltpu.VMEM((seq, 4 * width), f32),
            pltpu.VMEM((pairs, 2 * seq, seq), bf16),
            pltpu.VMEM((pairs, 2 * seq, seq), f32),
            pltpu.VMEM((seq, width), f32),
            pltpu.VMEM((seq, width), bf16),
            pltpu.SemaphoreType.DMA((10,)),
        ],
        compiler_params=pltpu.CompilerParams(vmem_limit_bytes=64 * 1024 * 1024),
        cost_estimate=pl.CostEstimate(flops=1_200_000_000, bytes_accessed=4_500_000, transcendentals=700_000),
        name="item_grad",
    )(length, *loaded)


def sum_rows(rows_ref, bucket):
    total = jnp.zeros((bucket.shape[0], rows_ref.shape[2]), f32)
    for member in range(rows_ref.shape[0]):
        ids = rows_ref[member, CAP:, :CAP].astype(f32)
        slot_id = ids[0:1] * ID_BASE + ids[1:2]
        slot_id = jnp.where(ids[2:3] > 0.5, slot_id, -1.0).astype(jnp.int32)
        chosen = jnp.where(bucket == slot_id, 1.0, 0.0).astype(bf16)
        total = total + dot(chosen, rows_ref[member, :CAP, :])
    return total


def hot_kernel(cores, first, base_ref, rows_ref, out_ref):
    z_size = out_ref.shape[0]
    place = lax.broadcasted_iota(jnp.int32, (z_size * HOT_DEV, CAP), 0)
    z = place // HOT_DEV + first
    z = jnp.where(z >= z_size, z - z_size, z)
    bucket = z * (HOT_DEV * cores) + place % HOT_DEV + base_ref[0]
    out_ref[...] = sum_rows(rows_ref, bucket).reshape(out_ref.shape).astype(bf16)


def hot_call(z_size, cores, first, base, rows):
    whole = pl.BlockSpec(memory_space=pltpu.VMEM)
    return pl.pallas_call(
        functools.partial(hot_kernel, cores, first),
        in_specs=[pl.BlockSpec(memory_space=pltpu.SMEM), whole],
        out_specs=whole,
        out_shape=jax.ShapeDtypeStruct((z_size, HOT_DEV, rows.shape[2]), bf16),
        compiler_params=pltpu.CompilerParams(vmem_limit_bytes=16 * 1024 * 1024),
        cost_estimate=pl.CostEstimate(flops=80_000_000, bytes_accessed=800_000, transcendentals=0),
        name="hot_sum",
    )(base, rows)


def cold_kernel(rows_ref, out_ref):
    out_ref[...] = sum_rows(rows_ref, lax.broadcasted_iota(jnp.int32, (COLD_DEV, CAP), 0))


def cold_call(rows):
    whole = pl.BlockSpec(memory_space=pltpu.VMEM)
    return pl.pallas_call(
        cold_kernel,
        in_specs=[whole],
        out_specs=whole,
        out_shape=jax.ShapeDtypeStruct((COLD_DEV, rows.shape[2]), f32),
        compiler_params=pltpu.CompilerParams(vmem_limit_bytes=16 * 1024 * 1024),
        cost_estimate=pl.CostEstimate(flops=40_000_000, bytes_accessed=600_000, transcendentals=0),
        name="cold_sum",
    )(rows)


def shards(embeddings, lengths, cotangent, w_proj, w_out, routes, hot_ids, cold_ids):
    owners = lax.axis_size("table")
    z_size, cores = lax.axis_size("z"), lax.axis_size("core")
    seq, width = embeddings.shape[1:]
    hot_rows, cold_rows = item_call(
        owners, lengths, embeddings.reshape(seq, width), cotangent.reshape(seq, width), w_proj, w_out,
        routes.reshape(1, seq), hot_ids, cold_ids,
    )
    cold_grad = cold_call(lax.all_to_all(cold_rows, "table", 0, 0))
    gathered = lax.all_gather(hot_rows, ("y", "core"))
    base = lax.axis_index("y") * (z_size * cores * HOT_DEV) + lax.axis_index("core") * HOT_DEV
    first = z_size * 5 // 8
    order = [(first + i) % z_size for i in range(z_size)]
    partial = hot_call(z_size, cores, first, base.reshape(1).astype(jnp.int32), gathered)
    parts = lax.all_to_all(partial, "z", 0, 0, axis_index_groups=[order])
    share = jnp.sum(parts.astype(f32), axis=0)
    hot_grad = lax.psum(share, "table")
    return (hot_grad, cold_grad)


def solution(mesh):
    dp, table = mesh.devices.shape
    cores, y_size = 2, 4
    fine = Mesh(mesh.devices.reshape(y_size, dp // (y_size * cores), cores, table), ("y", "z", "core", "table"))
    every = ("y", "z", "core", "table")
    return jax.shard_map(
        shards,
        mesh=fine,
        in_specs=(
            P(every, None, None),
            P(every),
            P(every, None, None),
            P(),
            P(),
            P(every, None, None),
            P(every, None),
            P(every, None),
        ),
        out_specs=(P(("y", "z", "core"), None), P(every, None)),
        check_vma=False,
    )
```

```python
import functools

import jax
import jax.numpy as jnp
from jax import lax
from jax.experimental import pallas as pl
from jax.experimental.pallas import tpu as pltpu
from jax.sharding import Mesh
from jax.sharding import PartitionSpec as P

HEAD_DIM = 64
HOT_DEV = 4
COLD_DEV = 128
CAP = 64
ID_ROWS = 16
ID_BASE = 32
PAIR = 2 * HEAD_DIM

epsilon = 1e-06
bf16 = jnp.bfloat16
f32 = jnp.float32


def dot(a, b, contract=((1,), (0,))):
    return lax.dot_general(a, b, (contract, ((), ())), preferred_element_type=f32)


def sigmoid(v):
    return 0.5 * jnp.tanh(0.5 * v) + 0.5


def item_kernel(owners, *refs):
    length_ref, me_ref, emb_hbm, cot_hbm, w_proj_hbm, w_out_hbm, routes_hbm, hot_hbm, cold_hbm = refs[:9]
    outs = refs[9 : 10 + owners]
    emb_ref, cot_ref, w_proj_ref, w_out_ref, routes_ref, hot_ref, cold_ref = refs[10 + owners : 17 + owners]
    proj, slope, weight, factor, attended, heads_grad, sems = refs[17 + owners :]
    seq, width = emb_ref.shape
    pairs = width // PAIR
    length = length_ref[0]

    loads = [(emb_hbm, emb_ref)]
    for part in (2, 3, 1, 0):
        cols = pl.ds(part * width, width)
        loads.append((w_proj_hbm.at[:, cols], w_proj_ref.at[:, cols]))
    loads += [(cot_hbm, cot_ref), (w_out_hbm, w_out_ref), (routes_hbm, routes_ref), (hot_hbm, hot_ref), (cold_hbm, cold_ref)]
    loads = [pltpu.make_async_copy(src, dst, sems.at[i]) for i, (src, dst) in enumerate(loads)]
    for load in loads:
        load.start()

    loads[0].wait()
    x = emb_ref[...].astype(f32)
    root = lax.rsqrt(jnp.mean(x * x, axis=1, keepdims=True) + epsilon)
    xn = x * root
    normed = xn.astype(bf16)
    for step, part in enumerate((2, 3, 1, 0)):
        cols = slice(part * width, (part + 1) * width)
        loads[1 + step].wait()
        pre = dot(normed, w_proj_ref[:, cols])
        gate = sigmoid(pre)
        act = pre * gate
        slope[:, cols] = gate + act * (1.0 - gate)
        scale = HEAD_DIM ** (-0.5) if part == 2 else 1.0
        proj[:, cols] = (act.astype(bf16) * jnp.asarray(scale, bf16))

    rows = lax.broadcasted_iota(jnp.int32, (seq, seq), 0)
    lanes = lax.broadcasted_iota(jnp.int32, (seq, seq), 1)
    inverse = 1.0 / jnp.full((seq, seq), length, jnp.int32).astype(f32)
    mask = jnp.where((lanes <= rows) & (rows < length), inverse, 0.0)
    low = lax.broadcasted_iota(jnp.int32, (seq, PAIR), 1) < HEAD_DIM

    def split_heads(block):
        zero = jnp.zeros_like(block)
        return jnp.concatenate([jnp.where(low, block, zero), jnp.where(low, zero, block)], axis=0)

    def join_heads(block):
        return jnp.where(low, block[:seq], block[seq:])

    def part_of(part, pair):
        return proj[:, part * width + pair * PAIR : part * width + (pair + 1) * PAIR]

    for pair in range(pairs):
        scores = dot(split_heads(part_of(2, pair)), part_of(3, pair), ((1,), (1,)))
        for head in range(2):
            score = scores[head * seq : (head + 1) * seq]
            gate = sigmoid(score)
            act = score * gate
            weight[pair, head * seq : (head + 1) * seq, :] = (act * mask).astype(bf16)
            factor[pair, head * seq : (head + 1) * seq, :] = (gate + act * (1.0 - gate)) * mask
        attended[:, pair * PAIR : (pair + 1) * PAIR] = join_heads(dot(weight[pair], part_of(1, pair)))

    loads[5].wait()
    loads[6].wait()
    att = attended[...]
    att_root = lax.rsqrt(jnp.mean(att * att, axis=1, keepdims=True) + epsilon)
    att_n = att * att_root
    mixed_grad = dot(cot_ref[...], w_out_ref[...], ((1,), (1,))).astype(bf16).astype(f32)
    gate_part = proj[:, :width].astype(f32)
    gate_grad = (mixed_grad * att_n).astype(bf16).astype(f32)
    proj[:, :width] = (gate_grad * slope[:, :width]).astype(bf16)
    att_n_grad = mixed_grad * gate_part
    inner = jnp.mean(att_n_grad * att_n, axis=1, keepdims=True)
    heads_grad[...] = (att_root * (att_n_grad - att_n * inner)).astype(bf16)

    for pair in range(pairs):
        query, key, value = part_of(2, pair), part_of(3, pair), part_of(1, pair)
        grad_split = split_heads(heads_grad[:, pair * PAIR : (pair + 1) * PAIR])
        weight_grad = dot(grad_split, value, ((1,), (1,))).astype(bf16).astype(f32)
        score_grad = (weight_grad * factor[pair]).astype(bf16)
        value_grad = dot(weight[pair], grad_split, ((0,), (0,)))
        query_grad = join_heads(dot(score_grad, key)) * HEAD_DIM ** (-0.5)
        key_grad = dot(score_grad, split_heads(query), ((0,), (0,)))
        for part, grad in ((1, value_grad), (2, query_grad), (3, key_grad)):
            cols = slice(part * width + pair * PAIR, part * width + (pair + 1) * PAIR)
            proj[:, cols] = (grad.astype(bf16).astype(f32) * slope[:, cols]).astype(bf16)

    normed_grad = dot(proj[...], w_proj_ref[...], ((1,), (1,))).astype(bf16).astype(f32)
    inner = jnp.mean(normed_grad * xn, axis=1, keepdims=True)
    total = root * (normed_grad - xn * inner) + cot_ref[...].astype(f32)
    valid = lax.broadcasted_iota(jnp.int32, (seq, width), 0) < length
    grad_rows = jnp.where(valid, total, 0.0).astype(bf16)

    for load in loads[7:]:
        load.wait()
    route = routes_ref[...]
    bucket = jnp.where(route == owners, hot_ref[...], cold_ref[...])
    kind = lax.broadcasted_iota(jnp.int32, (ID_ROWS, seq), 0)
    shift = route - me_ref[0]
    shift = jnp.where(route == owners, owners, jnp.where(shift < 0, shift + owners, shift))
    named = kind == shift
    before = jnp.where(rows < lanes, 1.0, 0.0).astype(bf16)
    place = dot(jnp.where(named, 1.0, 0.0).astype(bf16), before).astype(jnp.int32)
    place = jnp.where(named, place, -1)
    high = lax.shift_right_logical(bucket, 5).astype(f32)
    rest = (bucket & (ID_BASE - 1)).astype(f32)
    ids = jnp.where(kind == 0, high, jnp.where(kind == 1, rest, jnp.where(kind == 2, 1.0, 0.0))).astype(bf16)
    slots = lax.broadcasted_iota(jnp.int32, (CAP, seq), 0)
    for step, out in enumerate(outs):
        chosen = jnp.where(slots == place[step : step + 1], 1.0, 0.0).astype(bf16)
        out[:CAP, :] = dot(chosen, grad_rows).astype(bf16)
        slot_ids = dot(ids, chosen, ((1,), (1,)))
        out[CAP:, :] = jnp.zeros((ID_ROWS, width), bf16)
        out[CAP:, :PAIR] = jnp.concatenate([slot_ids, jnp.zeros((ID_ROWS, PAIR - CAP), f32)], axis=1).astype(bf16)


def item_call(owners, length, me, emb, cot, w_proj, w_out, routes, hot_ids, cold_ids):
    seq, width = emb.shape
    pairs = width // PAIR
    whole = pl.BlockSpec(memory_space=pltpu.VMEM)
    loaded = (emb, cot, w_proj, w_out, routes, hot_ids, cold_ids)
    return pl.pallas_call(
        functools.partial(item_kernel, owners),
        in_specs=[pl.BlockSpec(memory_space=pltpu.SMEM)] * 2 + [pl.BlockSpec(memory_space=pltpu.HBM)] * 7,
        out_specs=[whole] * (owners + 1),
        out_shape=[jax.ShapeDtypeStruct((CAP + ID_ROWS, width), bf16)] * (owners + 1),
        scratch_shapes=[pltpu.VMEM(a.shape, a.dtype) for a in loaded]
        + [
            pltpu.VMEM((seq, 4 * width), bf16),
            pltpu.VMEM((seq, 4 * width), f32),
            pltpu.VMEM((pairs, 2 * seq, seq), bf16),
            pltpu.VMEM((pairs, 2 * seq, seq), f32),
            pltpu.VMEM((seq, width), f32),
            pltpu.VMEM((seq, width), bf16),
            pltpu.SemaphoreType.DMA((10,)),
        ],
        compiler_params=pltpu.CompilerParams(vmem_limit_bytes=64 * 1024 * 1024),
        cost_estimate=pl.CostEstimate(flops=1_200_000_000, bytes_accessed=4_500_000, transcendentals=700_000),
        name="item_grad",
    )(length, me, *loaded)


def sum_rows(row_refs, bucket):
    total = jnp.zeros((bucket.shape[0], row_refs[0].shape[1]), f32)
    for rows_ref in row_refs:
        ids = rows_ref[CAP:, :CAP].astype(f32)
        slot_id = ids[0:1] * ID_BASE + ids[1:2]
        slot_id = jnp.where(ids[2:3] > 0.5, slot_id, -1.0).astype(jnp.int32)
        chosen = jnp.where(bucket == slot_id, 1.0, 0.0).astype(bf16)
        total = total + dot(chosen, rows_ref[:CAP, :])
    return total


def hot_kernel(cores, first, base_ref, rows_ref, out_ref):
    z_size = out_ref.shape[0]
    place = lax.broadcasted_iota(jnp.int32, (z_size * HOT_DEV, CAP), 0)
    z = place // HOT_DEV + first
    z = jnp.where(z >= z_size, z - z_size, z)
    bucket = z * (HOT_DEV * cores) + place % HOT_DEV + base_ref[0]
    out_ref[...] = sum_rows([rows_ref.at[i] for i in range(rows_ref.shape[0])], bucket).reshape(out_ref.shape).astype(bf16)


def hot_call(z_size, cores, first, base, rows):
    whole = pl.BlockSpec(memory_space=pltpu.VMEM)
    return pl.pallas_call(
        functools.partial(hot_kernel, cores, first),
        in_specs=[pl.BlockSpec(memory_space=pltpu.SMEM), whole],
        out_specs=whole,
        out_shape=jax.ShapeDtypeStruct((z_size, HOT_DEV, rows.shape[2]), bf16),
        compiler_params=pltpu.CompilerParams(vmem_limit_bytes=16 * 1024 * 1024),
        cost_estimate=pl.CostEstimate(flops=80_000_000, bytes_accessed=800_000, transcendentals=0),
        name="hot_sum",
    )(base, rows)


def cold_kernel(*refs):
    refs[-1][...] = sum_rows(refs[:-1], lax.broadcasted_iota(jnp.int32, (COLD_DEV, CAP), 0))


def cold_call(rows):
    whole = pl.BlockSpec(memory_space=pltpu.VMEM)
    return pl.pallas_call(
        cold_kernel,
        in_specs=[whole] * len(rows),
        out_specs=whole,
        out_shape=jax.ShapeDtypeStruct((COLD_DEV, rows[0].shape[1]), f32),
        compiler_params=pltpu.CompilerParams(vmem_limit_bytes=16 * 1024 * 1024),
        cost_estimate=pl.CostEstimate(flops=40_000_000, bytes_accessed=600_000, transcendentals=0),
        name="cold_sum",
    )(*rows)


def shards(embeddings, lengths, cotangent, w_proj, w_out, routes, hot_ids, cold_ids):
    owners = lax.axis_size("table")
    z_size, cores = lax.axis_size("z"), lax.axis_size("core")
    seq, width = embeddings.shape[1:]
    me = lax.axis_index("table").reshape(1).astype(jnp.int32)
    own_rows, *sent, hot_rows = item_call(
        owners, lengths, me, embeddings.reshape(seq, width), cotangent.reshape(seq, width), w_proj, w_out,
        routes.reshape(1, seq), hot_ids, cold_ids,
    )
    gathered = lax.all_gather(hot_rows, ("y", "core"))
    base = lax.axis_index("y") * (z_size * cores * HOT_DEV) + lax.axis_index("core") * HOT_DEV
    first = z_size * 5 // 8
    order = [(first + i) % z_size for i in range(z_size)]
    partial = hot_call(z_size, cores, first, base.reshape(1).astype(jnp.int32), gathered)
    partial, sent = lax.optimization_barrier((partial, sent))
    parts = lax.all_to_all(partial, "z", 0, 0, axis_index_groups=[order])
    received = [
        lax.ppermute(rows, "table", [(i, (i + step) % owners) for i in range(owners)])
        for step, rows in enumerate(sent, start=1)
    ]
    cold_grad = cold_call([*received, own_rows])
    share = jnp.sum(parts.astype(f32), axis=0)
    hot_grad = lax.psum(share, "table")
    return (hot_grad, cold_grad)


def solution(mesh):
    dp, table = mesh.devices.shape
    cores, y_size = 2, 4
    fine = Mesh(mesh.devices.reshape(y_size, dp // (y_size * cores), cores, table), ("y", "z", "core", "table"))
    every = ("y", "z", "core", "table")
    return jax.shard_map(
        shards,
        mesh=fine,
        in_specs=(
            P(every, None, None),
            P(every),
            P(every, None, None),
            P(),
            P(),
            P(every, None, None),
            P(every, None),
            P(every, None),
        ),
        out_specs=(P(("y", "z", "core"), None), P(every, None)),
        check_vma=False,
    )
```

```python
import functools

import jax
import jax.numpy as jnp
from jax import lax
from jax.experimental import pallas as pl
from jax.experimental.pallas import tpu as pltpu
from jax.sharding import Mesh
from jax.sharding import PartitionSpec as P

HEAD_DIM = 64
HOT_DEV = 4
COLD_DEV = 128
CAP = 64
ID_ROWS = 16
ID_BASE = 32
PAIR = 2 * HEAD_DIM

epsilon = 1e-06
bf16 = jnp.bfloat16
f32 = jnp.float32


def dot(a, b, contract=((1,), (0,))):
    return lax.dot_general(a, b, (contract, ((), ())), preferred_element_type=f32)


def sigmoid(v):
    return 0.5 * jnp.tanh(0.5 * v) + 0.5


def item_kernel(owners, *refs):
    length_ref, me_ref, emb_hbm, cot_hbm, w_proj_hbm, w_out_hbm, routes_hbm, hot_hbm, cold_hbm = refs[:9]
    outs = refs[9 : 10 + owners]
    emb_ref, cot_ref, w_proj_ref, w_out_ref, routes_ref, hot_ref, cold_ref = refs[10 + owners : 17 + owners]
    proj, slope, weight, factor, attended, heads_grad, sems = refs[17 + owners :]
    seq, width = emb_ref.shape
    pairs = width // PAIR
    length = length_ref[0]

    loads = [(emb_hbm, emb_ref)]
    for part in (2, 3, 1, 0):
        cols = pl.ds(part * width, width)
        loads.append((w_proj_hbm.at[:, cols], w_proj_ref.at[:, cols]))
    loads += [(cot_hbm, cot_ref), (w_out_hbm, w_out_ref), (routes_hbm, routes_ref), (hot_hbm, hot_ref), (cold_hbm, cold_ref)]
    loads = [pltpu.make_async_copy(src, dst, sems.at[i]) for i, (src, dst) in enumerate(loads)]
    for load in loads:
        load.start()

    loads[0].wait()
    x = emb_ref[...].astype(f32)
    root = lax.rsqrt(jnp.mean(x * x, axis=1, keepdims=True) + epsilon)
    xn = x * root
    normed = xn.astype(bf16)
    for step, part in enumerate((2, 3, 1, 0)):
        cols = slice(part * width, (part + 1) * width)
        loads[1 + step].wait()
        pre = dot(normed, w_proj_ref[:, cols])
        gate = sigmoid(pre)
        act = pre * gate
        slope[:, cols] = gate + act * (1.0 - gate)
        scale = HEAD_DIM ** (-0.5) if part == 2 else 1.0
        proj[:, cols] = (act.astype(bf16) * jnp.asarray(scale, bf16))

    rows = lax.broadcasted_iota(jnp.int32, (seq, seq), 0)
    lanes = lax.broadcasted_iota(jnp.int32, (seq, seq), 1)
    inverse = 1.0 / jnp.full((seq, seq), length, jnp.int32).astype(f32)
    mask = jnp.where((lanes <= rows) & (rows < length), inverse, 0.0)
    low = lax.broadcasted_iota(jnp.int32, (seq, PAIR), 1) < HEAD_DIM

    def split_heads(block):
        zero = jnp.zeros_like(block)
        return jnp.concatenate([jnp.where(low, block, zero), jnp.where(low, zero, block)], axis=0)

    def join_heads(block):
        return jnp.where(low, block[:seq], block[seq:])

    def part_of(part, pair):
        return proj[:, part * width + pair * PAIR : part * width + (pair + 1) * PAIR]

    for pair in range(pairs):
        scores = dot(split_heads(part_of(2, pair)), part_of(3, pair), ((1,), (1,)))
        for head in range(2):
            score = scores[head * seq : (head + 1) * seq]
            gate = sigmoid(score)
            act = score * gate
            weight[pair, head * seq : (head + 1) * seq, :] = (act * mask).astype(bf16)
            factor[pair, head * seq : (head + 1) * seq, :] = (gate + act * (1.0 - gate)) * mask
        attended[:, pair * PAIR : (pair + 1) * PAIR] = join_heads(dot(weight[pair], part_of(1, pair)))

    loads[5].wait()
    loads[6].wait()
    att = attended[...]
    att_root = lax.rsqrt(jnp.mean(att * att, axis=1, keepdims=True) + epsilon)
    att_n = att * att_root
    mixed_grad = dot(cot_ref[...], w_out_ref[...], ((1,), (1,))).astype(bf16).astype(f32)
    gate_part = proj[:, :width].astype(f32)
    gate_grad = (mixed_grad * att_n).astype(bf16).astype(f32)
    proj[:, :width] = (gate_grad * slope[:, :width]).astype(bf16)
    att_n_grad = mixed_grad * gate_part
    inner = jnp.mean(att_n_grad * att_n, axis=1, keepdims=True)
    heads_grad[...] = (att_root * (att_n_grad - att_n * inner)).astype(bf16)

    for pair in range(pairs):
        query, key, value = part_of(2, pair), part_of(3, pair), part_of(1, pair)
        grad_split = split_heads(heads_grad[:, pair * PAIR : (pair + 1) * PAIR])
        weight_grad = dot(grad_split, value, ((1,), (1,))).astype(bf16).astype(f32)
        score_grad = (weight_grad * factor[pair]).astype(bf16)
        value_grad = dot(weight[pair], grad_split, ((0,), (0,)))
        query_grad = join_heads(dot(score_grad, key)) * HEAD_DIM ** (-0.5)
        key_grad = dot(score_grad, split_heads(query), ((0,), (0,)))
        for part, grad in ((1, value_grad), (2, query_grad), (3, key_grad)):
            cols = slice(part * width + pair * PAIR, part * width + (pair + 1) * PAIR)
            proj[:, cols] = (grad.astype(bf16).astype(f32) * slope[:, cols]).astype(bf16)

    normed_grad = dot(proj[...], w_proj_ref[...], ((1,), (1,))).astype(bf16).astype(f32)
    inner = jnp.mean(normed_grad * xn, axis=1, keepdims=True)
    total = root * (normed_grad - xn * inner) + cot_ref[...].astype(f32)
    valid = lax.broadcasted_iota(jnp.int32, (seq, width), 0) < length
    grad_rows = jnp.where(valid, total, 0.0).astype(bf16)

    for load in loads[7:]:
        load.wait()
    route = routes_ref[...]
    bucket = jnp.where(route == owners, hot_ref[...], cold_ref[...])
    kind = lax.broadcasted_iota(jnp.int32, (ID_ROWS, seq), 0)
    shift = route - me_ref[0]
    shift = jnp.where(route == owners, owners, jnp.where(shift < 0, shift + owners, shift))
    named = kind == shift
    before = jnp.where(rows < lanes, 1.0, 0.0).astype(bf16)
    place = dot(jnp.where(named, 1.0, 0.0).astype(bf16), before).astype(jnp.int32)
    place = jnp.where(named, place, -1)
    high = lax.shift_right_logical(bucket, 5).astype(f32)
    rest = (bucket & (ID_BASE - 1)).astype(f32)
    ids = jnp.where(kind == 0, high, jnp.where(kind == 1, rest, jnp.where(kind == 2, 1.0, 0.0))).astype(bf16)
    slots = lax.broadcasted_iota(jnp.int32, (CAP, seq), 0)
    for step, out in enumerate(outs):
        chosen = jnp.where(slots == place[step : step + 1], 1.0, 0.0).astype(bf16)
        out[:CAP, :] = dot(chosen, grad_rows).astype(bf16)
        slot_ids = dot(ids, chosen, ((1,), (1,)))
        out[CAP:, :] = jnp.zeros((ID_ROWS, width), bf16)
        out[CAP:, :PAIR] = jnp.concatenate([slot_ids, jnp.zeros((ID_ROWS, PAIR - CAP), f32)], axis=1).astype(bf16)


def item_call(owners, length, me, emb, cot, w_proj, w_out, routes, hot_ids, cold_ids):
    seq, width = emb.shape
    pairs = width // PAIR
    whole = pl.BlockSpec(memory_space=pltpu.VMEM)
    loaded = (emb, cot, w_proj, w_out, routes, hot_ids, cold_ids)
    return pl.pallas_call(
        functools.partial(item_kernel, owners),
        in_specs=[pl.BlockSpec(memory_space=pltpu.SMEM)] * 2 + [pl.BlockSpec(memory_space=pltpu.HBM)] * 7,
        out_specs=[whole] * (owners + 1),
        out_shape=[jax.ShapeDtypeStruct((CAP + ID_ROWS, width), bf16)] * (owners + 1),
        scratch_shapes=[pltpu.VMEM(a.shape, a.dtype) for a in loaded]
        + [
            pltpu.VMEM((seq, 4 * width), bf16),
            pltpu.VMEM((seq, 4 * width), f32),
            pltpu.VMEM((pairs, 2 * seq, seq), bf16),
            pltpu.VMEM((pairs, 2 * seq, seq), f32),
            pltpu.VMEM((seq, width), f32),
            pltpu.VMEM((seq, width), bf16),
            pltpu.SemaphoreType.DMA((10,)),
        ],
        compiler_params=pltpu.CompilerParams(vmem_limit_bytes=64 * 1024 * 1024),
        cost_estimate=pl.CostEstimate(flops=1_200_000_000, bytes_accessed=4_500_000, transcendentals=700_000),
        name="item_grad",
    )(length, me, *loaded)


def sum_rows(row_refs, bucket):
    total = jnp.zeros((bucket.shape[0], row_refs[0].shape[1]), f32)
    for rows_ref in row_refs:
        ids = rows_ref[CAP:, :CAP].astype(f32)
        slot_id = ids[0:1] * ID_BASE + ids[1:2]
        slot_id = jnp.where(ids[2:3] > 0.5, slot_id, -1.0).astype(jnp.int32)
        chosen = jnp.where(bucket == slot_id, 1.0, 0.0).astype(bf16)
        total = total + dot(chosen, rows_ref[:CAP, :])
    return total


def hot_kernel(cores, first, base_ref, rows_ref, out_ref):
    z_size = out_ref.shape[0]
    place = lax.broadcasted_iota(jnp.int32, (z_size * HOT_DEV, CAP), 0)
    z = first - place // HOT_DEV
    z = jnp.where(z < 0, z + z_size, z)
    bucket = z * (HOT_DEV * cores) + place % HOT_DEV + base_ref[0]
    out_ref[...] = sum_rows([rows_ref.at[i] for i in range(rows_ref.shape[0])], bucket).reshape(out_ref.shape).astype(bf16)


def hot_call(z_size, cores, first, base, rows):
    whole = pl.BlockSpec(memory_space=pltpu.VMEM)
    return pl.pallas_call(
        functools.partial(hot_kernel, cores, first),
        in_specs=[pl.BlockSpec(memory_space=pltpu.SMEM), whole],
        out_specs=whole,
        out_shape=jax.ShapeDtypeStruct((z_size, HOT_DEV, rows.shape[2]), bf16),
        compiler_params=pltpu.CompilerParams(vmem_limit_bytes=16 * 1024 * 1024),
        cost_estimate=pl.CostEstimate(flops=80_000_000, bytes_accessed=800_000, transcendentals=0),
        name="hot_sum",
    )(base, rows)


def cold_kernel(*refs):
    refs[-1][...] = sum_rows(refs[:-1], lax.broadcasted_iota(jnp.int32, (COLD_DEV, CAP), 0))


def cold_call(rows):
    whole = pl.BlockSpec(memory_space=pltpu.VMEM)
    return pl.pallas_call(
        cold_kernel,
        in_specs=[whole] * len(rows),
        out_specs=whole,
        out_shape=jax.ShapeDtypeStruct((COLD_DEV, rows[0].shape[1]), f32),
        compiler_params=pltpu.CompilerParams(vmem_limit_bytes=16 * 1024 * 1024),
        cost_estimate=pl.CostEstimate(flops=40_000_000, bytes_accessed=600_000, transcendentals=0),
        name="cold_sum",
    )(*rows)


def spread_kernel(parts_ref, out_ref):
    total = parts_ref[0].astype(f32)
    for i in range(1, parts_ref.shape[0]):
        total = total + parts_ref[i].astype(f32)
    for i in range(out_ref.shape[0]):
        out_ref[i] = total


def spread_call(owners, parts):
    whole = pl.BlockSpec(memory_space=pltpu.VMEM)
    return pl.pallas_call(
        spread_kernel,
        in_specs=[whole],
        out_specs=whole,
        out_shape=jax.ShapeDtypeStruct((owners,) + parts.shape[1:], f32),
        compiler_params=pltpu.CompilerParams(vmem_limit_bytes=16 * 1024 * 1024),
        cost_estimate=pl.CostEstimate(flops=70_000, bytes_accessed=160_000, transcendentals=0),
        name="spread",
    )(parts)


def shards(embeddings, lengths, cotangent, w_proj, w_out, routes, hot_ids, cold_ids):
    owners = lax.axis_size("table")
    z_size, cores = lax.axis_size("z"), lax.axis_size("core")
    seq, width = embeddings.shape[1:]
    me = lax.axis_index("table").reshape(1).astype(jnp.int32)
    own_rows, *sent, hot_rows = item_call(
        owners, lengths, me, embeddings.reshape(seq, width), cotangent.reshape(seq, width), w_proj, w_out,
        routes.reshape(1, seq), hot_ids, cold_ids,
    )
    gathered = lax.all_gather(hot_rows, ("y", "core"))
    base = lax.axis_index("y") * (z_size * cores * HOT_DEV) + lax.axis_index("core") * HOT_DEV
    first = z_size * 5 // 8
    order = [(first - i) % z_size for i in range(z_size)]
    partial = hot_call(z_size, cores, first, base.reshape(1).astype(jnp.int32), gathered)
    partial, sent = lax.optimization_barrier((partial, sent))
    parts = lax.all_to_all(partial, "z", 0, 0, axis_index_groups=[order])
    received = [
        lax.ppermute(rows, "table", [(i, (i + step) % owners) for i in range(owners)])
        for step, rows in enumerate(sent, start=1)
    ]
    cold_grad = cold_call([*received, own_rows])
    last = [(owners - 1 + i) % owners for i in range(owners)]
    copies = lax.all_to_all(spread_call(owners, parts), "table", 0, 0, axis_index_groups=[last])
    hot_grad = jnp.sum(copies, axis=0)
    return (hot_grad, cold_grad)


def solution(mesh):
    dp, table = mesh.devices.shape
    cores, y_size = 2, 4
    fine = Mesh(mesh.devices.reshape(y_size, dp // (y_size * cores), cores, table), ("y", "z", "core", "table"))
    every = ("y", "z", "core", "table")
    return jax.shard_map(
        shards,
        mesh=fine,
        in_specs=(
            P(every, None, None),
            P(every),
            P(every, None, None),
            P(),
            P(),
            P(every, None, None),
            P(every, None),
            P(every, None),
        ),
        out_specs=(P(("y", "z", "core"), None), P(every, None)),
        check_vma=False,
    )
```

```python
import functools

import jax
import jax.numpy as jnp
from jax import lax
from jax.experimental import pallas as pl
from jax.experimental.pallas import tpu as pltpu
from jax.sharding import Mesh
from jax.sharding import PartitionSpec as P

HEAD_DIM = 64
HOT_DEV = 4
COLD_DEV = 128
CAP = 64
ID_ROWS = 16
ID_BASE = 32
PAIR = 2 * HEAD_DIM

epsilon = 1e-06
bf16 = jnp.bfloat16
f32 = jnp.float32


def dot(a, b, contract=((1,), (0,))):
    return lax.dot_general(a, b, (contract, ((), ())), preferred_element_type=f32)


def sigmoid(v):
    return 0.5 * jnp.tanh(0.5 * v) + 0.5


def item_kernel(owners, *refs):
    length_ref, me_ref, emb_hbm, cot_hbm, w_proj_hbm, w_out_hbm, routes_hbm, hot_hbm, cold_hbm = refs[:9]
    outs = refs[9 : 10 + owners]
    emb_ref, cot_ref, w_proj_ref, w_out_ref, routes_ref, hot_ref, cold_ref = refs[10 + owners : 17 + owners]
    proj, slope, weight, factor, attended, heads_grad, sems = refs[17 + owners :]
    seq, width = emb_ref.shape
    pairs = width // PAIR
    length = length_ref[0]

    loads = [(emb_hbm, emb_ref)]
    for part in (2, 3, 1, 0):
        cols = pl.ds(part * width, width)
        loads.append((w_proj_hbm.at[:, cols], w_proj_ref.at[:, cols]))
    loads += [(cot_hbm, cot_ref), (w_out_hbm, w_out_ref), (routes_hbm, routes_ref), (hot_hbm, hot_ref), (cold_hbm, cold_ref)]
    loads = [pltpu.make_async_copy(src, dst, sems.at[i]) for i, (src, dst) in enumerate(loads)]
    for load in loads:
        load.start()

    loads[0].wait()
    x = emb_ref[...].astype(f32)
    root = lax.rsqrt(jnp.mean(x * x, axis=1, keepdims=True) + epsilon)
    xn = x * root
    normed = xn.astype(bf16)
    for step, part in enumerate((2, 3, 1, 0)):
        cols = slice(part * width, (part + 1) * width)
        loads[1 + step].wait()
        pre = dot(normed, w_proj_ref[:, cols])
        gate = sigmoid(pre)
        act = pre * gate
        slope[:, cols] = gate + act * (1.0 - gate)
        scale = HEAD_DIM ** (-0.5) if part == 2 else 1.0
        proj[:, cols] = (act.astype(bf16) * jnp.asarray(scale, bf16))

    rows = lax.broadcasted_iota(jnp.int32, (seq, seq), 0)
    lanes = lax.broadcasted_iota(jnp.int32, (seq, seq), 1)
    inverse = 1.0 / jnp.full((seq, seq), length, jnp.int32).astype(f32)
    mask = jnp.where((lanes <= rows) & (rows < length), inverse, 0.0)
    low = lax.broadcasted_iota(jnp.int32, (seq, PAIR), 1) < HEAD_DIM

    def split_heads(block):
        zero = jnp.zeros_like(block)
        return jnp.concatenate([jnp.where(low, block, zero), jnp.where(low, zero, block)], axis=0)

    def join_heads(block):
        return jnp.where(low, block[:seq], block[seq:])

    def part_of(part, pair):
        return proj[:, part * width + pair * PAIR : part * width + (pair + 1) * PAIR]

    for pair in range(pairs):
        scores = dot(split_heads(part_of(2, pair)), part_of(3, pair), ((1,), (1,)))
        for head in range(2):
            score = scores[head * seq : (head + 1) * seq]
            gate = sigmoid(score)
            act = score * gate
            weight[pair, head * seq : (head + 1) * seq, :] = (act * mask).astype(bf16)
            factor[pair, head * seq : (head + 1) * seq, :] = (gate + act * (1.0 - gate)) * mask
        attended[:, pair * PAIR : (pair + 1) * PAIR] = join_heads(dot(weight[pair], part_of(1, pair)))

    loads[5].wait()
    loads[6].wait()
    att = attended[...]
    att_root = lax.rsqrt(jnp.mean(att * att, axis=1, keepdims=True) + epsilon)
    att_n = att * att_root
    mixed_grad = dot(cot_ref[...], w_out_ref[...], ((1,), (1,))).astype(bf16).astype(f32)
    gate_part = proj[:, :width].astype(f32)
    gate_grad = (mixed_grad * att_n).astype(bf16).astype(f32)
    proj[:, :width] = (gate_grad * slope[:, :width]).astype(bf16)
    att_n_grad = mixed_grad * gate_part
    inner = jnp.mean(att_n_grad * att_n, axis=1, keepdims=True)
    heads_grad[...] = (att_root * (att_n_grad - att_n * inner)).astype(bf16)

    for pair in range(pairs):
        query, key, value = part_of(2, pair), part_of(3, pair), part_of(1, pair)
        grad_split = split_heads(heads_grad[:, pair * PAIR : (pair + 1) * PAIR])
        weight_grad = dot(grad_split, value, ((1,), (1,))).astype(bf16).astype(f32)
        score_grad = (weight_grad * factor[pair]).astype(bf16)
        value_grad = dot(weight[pair], grad_split, ((0,), (0,)))
        query_grad = join_heads(dot(score_grad, key)) * HEAD_DIM ** (-0.5)
        key_grad = dot(score_grad, split_heads(query), ((0,), (0,)))
        for part, grad in ((1, value_grad), (2, query_grad), (3, key_grad)):
            cols = slice(part * width + pair * PAIR, part * width + (pair + 1) * PAIR)
            proj[:, cols] = (grad.astype(bf16).astype(f32) * slope[:, cols]).astype(bf16)

    normed_grad = dot(proj[...], w_proj_ref[...], ((1,), (1,))).astype(bf16).astype(f32)
    inner = jnp.mean(normed_grad * xn, axis=1, keepdims=True)
    total = root * (normed_grad - xn * inner) + cot_ref[...].astype(f32)
    valid = lax.broadcasted_iota(jnp.int32, (seq, width), 0) < length
    grad_rows = jnp.where(valid, total, 0.0).astype(bf16)

    for load in loads[7:]:
        load.wait()
    route = routes_ref[...]
    bucket = jnp.where(route == owners, hot_ref[...], cold_ref[...])
    kind = lax.broadcasted_iota(jnp.int32, (ID_ROWS, seq), 0)
    shift = route - me_ref[0]
    shift = jnp.where(route == owners, owners, jnp.where(shift < 0, shift + owners, shift))
    named = kind == shift
    before = jnp.where(rows < lanes, 1.0, 0.0).astype(bf16)
    place = dot(jnp.where(named, 1.0, 0.0).astype(bf16), before).astype(jnp.int32)
    place = jnp.where(named, place, -1)
    high = lax.shift_right_logical(bucket, 5).astype(f32)
    rest = (bucket & (ID_BASE - 1)).astype(f32)
    ids = jnp.where(kind == 0, high, jnp.where(kind == 1, rest, jnp.where(kind == 2, 1.0, 0.0))).astype(bf16)
    slots = lax.broadcasted_iota(jnp.int32, (CAP, seq), 0)
    for step, out in enumerate(outs):
        chosen = jnp.where(slots == place[step : step + 1], 1.0, 0.0).astype(bf16)
        sent = dot(chosen, grad_rows).astype(bf16)
        slot_ids = dot(ids, chosen, ((1,), (1,)))
        slot_ids = jnp.concatenate([slot_ids, jnp.zeros((ID_ROWS, PAIR - CAP), f32)], axis=1).astype(bf16)
        if step < owners:
            out[:CAP, :] = sent
            out[CAP:, :] = jnp.zeros((ID_ROWS, width), bf16)
            out[CAP:, :PAIR] = slot_ids
        else:
            piece = width // owners
            for block in range(out.shape[0]):
                start = block % owners * piece
                out[block, :CAP, :] = sent[:, start : start + piece]
                out[block, CAP:, :] = slot_ids


def item_call(owners, near, length, me, emb, cot, w_proj, w_out, routes, hot_ids, cold_ids):
    seq, width = emb.shape
    pairs = width // PAIR
    whole = pl.BlockSpec(memory_space=pltpu.VMEM)
    loaded = (emb, cot, w_proj, w_out, routes, hot_ids, cold_ids)
    return pl.pallas_call(
        functools.partial(item_kernel, owners),
        in_specs=[pl.BlockSpec(memory_space=pltpu.SMEM)] * 2 + [pl.BlockSpec(memory_space=pltpu.HBM)] * 7,
        out_specs=[whole] * (owners + 1),
        out_shape=[jax.ShapeDtypeStruct((CAP + ID_ROWS, width), bf16)] * owners
        + [jax.ShapeDtypeStruct((near * owners, CAP + ID_ROWS, width // owners), bf16)],
        scratch_shapes=[pltpu.VMEM(a.shape, a.dtype) for a in loaded]
        + [
            pltpu.VMEM((seq, 4 * width), bf16),
            pltpu.VMEM((seq, 4 * width), f32),
            pltpu.VMEM((pairs, 2 * seq, seq), bf16),
            pltpu.VMEM((pairs, 2 * seq, seq), f32),
            pltpu.VMEM((seq, width), f32),
            pltpu.VMEM((seq, width), bf16),
            pltpu.SemaphoreType.DMA((10,)),
        ],
        compiler_params=pltpu.CompilerParams(vmem_limit_bytes=64 * 1024 * 1024),
        cost_estimate=pl.CostEstimate(flops=1_200_000_000, bytes_accessed=4_500_000, transcendentals=700_000),
        name="item_grad",
    )(length, me, *loaded)


def sum_rows(row_refs, bucket):
    total = jnp.zeros((bucket.shape[0], row_refs[0].shape[1]), f32)
    for rows_ref in row_refs:
        ids = rows_ref[CAP:, :CAP].astype(f32)
        slot_id = ids[0:1] * ID_BASE + ids[1:2]
        slot_id = jnp.where(ids[2:3] > 0.5, slot_id, -1.0).astype(jnp.int32)
        chosen = jnp.where(bucket == slot_id, 1.0, 0.0).astype(bf16)
        total = total + dot(chosen, rows_ref[:CAP, :])
    return total


def hot_kernel(cores, first, base_ref, rows_ref, out_ref):
    z_size = out_ref.shape[0]
    place = lax.broadcasted_iota(jnp.int32, (z_size * HOT_DEV, CAP), 0)
    z = first - place // HOT_DEV
    z = jnp.where(z < 0, z + z_size, z)
    bucket = z * (HOT_DEV * cores) + place % HOT_DEV + base_ref[0]
    out_ref[...] = sum_rows([rows_ref.at[i] for i in range(rows_ref.shape[0])], bucket).reshape(out_ref.shape).astype(bf16)


def hot_call(z_size, cores, first, base, rows):
    whole = pl.BlockSpec(memory_space=pltpu.VMEM)
    return pl.pallas_call(
        functools.partial(hot_kernel, cores, first),
        in_specs=[pl.BlockSpec(memory_space=pltpu.SMEM), whole],
        out_specs=whole,
        out_shape=jax.ShapeDtypeStruct((z_size, HOT_DEV, rows.shape[2]), bf16),
        compiler_params=pltpu.CompilerParams(vmem_limit_bytes=16 * 1024 * 1024),
        cost_estimate=pl.CostEstimate(flops=80_000_000, bytes_accessed=800_000, transcendentals=0),
        name="hot_sum",
    )(base, rows)


def cold_kernel(*refs):
    refs[-1][...] = sum_rows(refs[:-1], lax.broadcasted_iota(jnp.int32, (COLD_DEV, CAP), 0))


def cold_call(rows):
    whole = pl.BlockSpec(memory_space=pltpu.VMEM)
    return pl.pallas_call(
        cold_kernel,
        in_specs=[whole] * len(rows),
        out_specs=whole,
        out_shape=jax.ShapeDtypeStruct((COLD_DEV, rows[0].shape[1]), f32),
        compiler_params=pltpu.CompilerParams(vmem_limit_bytes=16 * 1024 * 1024),
        cost_estimate=pl.CostEstimate(flops=40_000_000, bytes_accessed=600_000, transcendentals=0),
        name="cold_sum",
    )(*rows)


def spread_kernel(parts_ref, out_ref):
    total = parts_ref[0].astype(f32)
    for i in range(1, parts_ref.shape[0]):
        total = total + parts_ref[i].astype(f32)
    for i in range(out_ref.shape[0]):
        out_ref[i] = total


def spread_call(owners, parts):
    whole = pl.BlockSpec(memory_space=pltpu.VMEM)
    return pl.pallas_call(
        spread_kernel,
        in_specs=[whole],
        out_specs=whole,
        out_shape=jax.ShapeDtypeStruct((owners,) + parts.shape[1:], f32),
        compiler_params=pltpu.CompilerParams(vmem_limit_bytes=16 * 1024 * 1024),
        cost_estimate=pl.CostEstimate(flops=70_000, bytes_accessed=160_000, transcendentals=0),
        name="spread",
    )(parts)


def shards(embeddings, lengths, cotangent, w_proj, w_out, routes, hot_ids, cold_ids):
    owners = lax.axis_size("table")
    z_size, cores = lax.axis_size("z"), lax.axis_size("core")
    seq, width = embeddings.shape[1:]
    me = lax.axis_index("table").reshape(1).astype(jnp.int32)
    own_rows, *sent, hot_rows = item_call(
        owners, lax.axis_size("y") * cores, lengths, me, embeddings.reshape(seq, width), cotangent.reshape(seq, width), w_proj, w_out,
        routes.reshape(1, seq), hot_ids, cold_ids,
    )
    gathered = lax.all_to_all(hot_rows, ("y", "core", "table"), 0, 0)
    base = lax.axis_index("y") * (z_size * cores * HOT_DEV) + lax.axis_index("core") * HOT_DEV
    first = z_size * 5 // 8
    order = [(first - i) % z_size for i in range(z_size)]
    partial = hot_call(z_size, cores, first, base.reshape(1).astype(jnp.int32), gathered)
    partial, sent = lax.optimization_barrier((partial, sent))
    parts = lax.all_to_all(partial, "z", 0, 0, axis_index_groups=[order])
    received = [
        lax.ppermute(rows, "table", [(i, (i + step) % owners) for i in range(owners)])
        for step, rows in enumerate(sent, start=1)
    ]
    cold_grad = cold_call([*received, own_rows])
    copies = lax.all_to_all(spread_call(owners, parts), "table", 0, 0)
    hot_grad = jnp.transpose(copies, (1, 0, 2)).reshape(HOT_DEV, width)
    return (hot_grad, cold_grad)


def solution(mesh):
    dp, table = mesh.devices.shape
    cores, y_size = 2, 4
    fine = Mesh(mesh.devices.reshape(y_size, dp // (y_size * cores), cores, table), ("y", "z", "core", "table"))
    every = ("y", "z", "core", "table")
    return jax.shard_map(
        shards,
        mesh=fine,
        in_specs=(
            P(every, None, None),
            P(every),
            P(every, None, None),
            P(),
            P(),
            P(every, None, None),
            P(every, None),
            P(every, None),
        ),
        out_specs=(P(("y", "z", "core"), None), P(every, None)),
        check_vma=False,
    )
```

```python
import functools

import jax
import jax.numpy as jnp
from jax import lax
from jax.experimental import pallas as pl
from jax.experimental.pallas import tpu as pltpu
from jax.sharding import Mesh
from jax.sharding import PartitionSpec as P

HEAD_DIM = 64
HOT_DEV = 4
COLD_DEV = 128
CAP = 64
ID_ROWS = 16
ID_BASE = 32
PAIR = 2 * HEAD_DIM

epsilon = 1e-06
bf16 = jnp.bfloat16
f32 = jnp.float32


def dot(a, b, contract=((1,), (0,))):
    return lax.dot_general(a, b, (contract, ((), ())), preferred_element_type=f32)


def sigmoid(v):
    return 0.5 * jnp.tanh(0.5 * v) + 0.5


def item_kernel(owners, *refs):
    length_ref, me_ref, emb_hbm, cot_hbm, w_proj_hbm, w_out_hbm, routes_hbm, hot_hbm, cold_hbm = refs[:9]
    outs = refs[9 : 10 + owners]
    emb_ref, cot_ref, w_proj_ref, w_out_ref, routes_ref, hot_ref, cold_ref = refs[10 + owners : 17 + owners]
    proj, slope, weight, factor, attended, heads_grad, sems = refs[17 + owners :]
    seq, width = emb_ref.shape
    pairs = width // PAIR
    length = length_ref[0]

    loads = [(emb_hbm, emb_ref)]
    for part in (2, 3, 1, 0):
        cols = pl.ds(part * width, width)
        loads.append((w_proj_hbm.at[:, cols], w_proj_ref.at[:, cols]))
    loads += [(cot_hbm, cot_ref), (w_out_hbm, w_out_ref), (routes_hbm, routes_ref), (hot_hbm, hot_ref), (cold_hbm, cold_ref)]
    loads = [pltpu.make_async_copy(src, dst, sems.at[i]) for i, (src, dst) in enumerate(loads)]
    for load in loads:
        load.start()

    loads[0].wait()
    x = emb_ref[...].astype(f32)
    root = lax.rsqrt(jnp.mean(x * x, axis=1, keepdims=True) + epsilon)
    xn = x * root
    normed = xn.astype(bf16)
    for step, part in enumerate((2, 3, 1, 0)):
        cols = slice(part * width, (part + 1) * width)
        loads[1 + step].wait()
        pre = dot(normed, w_proj_ref[:, cols])
        gate = sigmoid(pre)
        act = pre * gate
        slope[:, cols] = gate + act * (1.0 - gate)
        scale = HEAD_DIM ** (-0.5) if part == 2 else 1.0
        proj[:, cols] = (act.astype(bf16) * jnp.asarray(scale, bf16))

    rows = lax.broadcasted_iota(jnp.int32, (seq, seq), 0)
    lanes = lax.broadcasted_iota(jnp.int32, (seq, seq), 1)
    inverse = 1.0 / jnp.full((seq, seq), length, jnp.int32).astype(f32)
    mask = jnp.where((lanes <= rows) & (rows < length), inverse, 0.0)
    low = lax.broadcasted_iota(jnp.int32, (seq, PAIR), 1) < HEAD_DIM

    def split_heads(block):
        zero = jnp.zeros_like(block)
        return jnp.concatenate([jnp.where(low, block, zero), jnp.where(low, zero, block)], axis=0)

    def join_heads(block):
        return jnp.where(low, block[:seq], block[seq:])

    def part_of(part, pair):
        return proj[:, part * width + pair * PAIR : part * width + (pair + 1) * PAIR]

    for pair in range(pairs):
        scores = dot(split_heads(part_of(2, pair)), part_of(3, pair), ((1,), (1,)))
        for head in range(2):
            score = scores[head * seq : (head + 1) * seq]
            gate = sigmoid(score)
            act = score * gate
            weight[pair, head * seq : (head + 1) * seq, :] = (act * mask).astype(bf16)
            factor[pair, head * seq : (head + 1) * seq, :] = (gate + act * (1.0 - gate)) * mask
        attended[:, pair * PAIR : (pair + 1) * PAIR] = join_heads(dot(weight[pair], part_of(1, pair)))

    loads[5].wait()
    loads[6].wait()
    att = attended[...]
    att_root = lax.rsqrt(jnp.mean(att * att, axis=1, keepdims=True) + epsilon)
    att_n = att * att_root
    mixed_grad = dot(cot_ref[...], w_out_ref[...], ((1,), (1,))).astype(bf16).astype(f32)
    gate_part = proj[:, :width].astype(f32)
    gate_grad = (mixed_grad * att_n).astype(bf16).astype(f32)
    proj[:, :width] = (gate_grad * slope[:, :width]).astype(bf16)
    att_n_grad = mixed_grad * gate_part
    inner = jnp.mean(att_n_grad * att_n, axis=1, keepdims=True)
    heads_grad[...] = (att_root * (att_n_grad - att_n * inner)).astype(bf16)

    for pair in range(pairs):
        query, key, value = part_of(2, pair), part_of(3, pair), part_of(1, pair)
        grad_split = split_heads(heads_grad[:, pair * PAIR : (pair + 1) * PAIR])
        weight_grad = dot(grad_split, value, ((1,), (1,))).astype(bf16).astype(f32)
        score_grad = (weight_grad * factor[pair]).astype(bf16)
        value_grad = dot(weight[pair], grad_split, ((0,), (0,)))
        query_grad = join_heads(dot(score_grad, key)) * HEAD_DIM ** (-0.5)
        key_grad = dot(score_grad, split_heads(query), ((0,), (0,)))
        for part, grad in ((1, value_grad), (2, query_grad), (3, key_grad)):
            cols = slice(part * width + pair * PAIR, part * width + (pair + 1) * PAIR)
            proj[:, cols] = (grad.astype(bf16).astype(f32) * slope[:, cols]).astype(bf16)

    normed_grad = dot(proj[...], w_proj_ref[...], ((1,), (1,))).astype(bf16).astype(f32)
    inner = jnp.mean(normed_grad * xn, axis=1, keepdims=True)
    total = root * (normed_grad - xn * inner) + cot_ref[...].astype(f32)
    valid = lax.broadcasted_iota(jnp.int32, (seq, width), 0) < length
    grad_rows = jnp.where(valid, total, 0.0).astype(bf16)

    for load in loads[7:]:
        load.wait()
    route = routes_ref[...]
    bucket = jnp.where(route == owners, hot_ref[...], cold_ref[...])
    kind = lax.broadcasted_iota(jnp.int32, (ID_ROWS, seq), 0)
    shift = route - me_ref[0]
    shift = jnp.where(route == owners, owners, jnp.where(shift < 0, shift + owners, shift))
    named = kind == shift
    before = jnp.where(rows < lanes, 1.0, 0.0).astype(bf16)
    place = dot(jnp.where(named, 1.0, 0.0).astype(bf16), before).astype(jnp.int32)
    place = jnp.where(named, place, -1)
    high = lax.shift_right_logical(bucket, 5).astype(f32)
    rest = (bucket & (ID_BASE - 1)).astype(f32)
    ids = jnp.where(kind == 0, high, jnp.where(kind == 1, rest, jnp.where(kind == 2, 1.0, 0.0))).astype(bf16)
    slots = lax.broadcasted_iota(jnp.int32, (CAP, seq), 0)
    for step, out in enumerate(outs):
        chosen = jnp.where(slots == place[step : step + 1], 1.0, 0.0).astype(bf16)
        sent = dot(chosen, grad_rows).astype(bf16)
        slot_ids = dot(ids, chosen, ((1,), (1,)))
        slot_ids = jnp.concatenate([slot_ids, jnp.zeros((ID_ROWS, PAIR - CAP), f32)], axis=1).astype(bf16)
        if step < owners:
            out[:CAP, :] = sent
            out[CAP:, :] = jnp.zeros((ID_ROWS, width), bf16)
            out[CAP:, :PAIR] = slot_ids
        else:
            piece = width // owners
            for block in range(out.shape[0]):
                start = (block + 1) % owners * piece
                out[block, :CAP, :] = sent[:, start : start + piece]
                out[block, CAP:, :] = slot_ids


def item_call(owners, near, length, me, emb, cot, w_proj, w_out, routes, hot_ids, cold_ids):
    seq, width = emb.shape
    pairs = width // PAIR
    whole = pl.BlockSpec(memory_space=pltpu.VMEM)
    loaded = (emb, cot, w_proj, w_out, routes, hot_ids, cold_ids)
    return pl.pallas_call(
        functools.partial(item_kernel, owners),
        in_specs=[pl.BlockSpec(memory_space=pltpu.SMEM)] * 2 + [pl.BlockSpec(memory_space=pltpu.HBM)] * 7,
        out_specs=[whole] * (owners + 1),
        out_shape=[jax.ShapeDtypeStruct((CAP + ID_ROWS, width), bf16)] * owners
        + [jax.ShapeDtypeStruct((near * owners, CAP + ID_ROWS, width // owners), bf16)],
        scratch_shapes=[pltpu.VMEM(a.shape, a.dtype) for a in loaded]
        + [
            pltpu.VMEM((seq, 4 * width), bf16),
            pltpu.VMEM((seq, 4 * width), f32),
            pltpu.VMEM((pairs, 2 * seq, seq), bf16),
            pltpu.VMEM((pairs, 2 * seq, seq), f32),
            pltpu.VMEM((seq, width), f32),
            pltpu.VMEM((seq, width), bf16),
            pltpu.SemaphoreType.DMA((10,)),
        ],
        compiler_params=pltpu.CompilerParams(vmem_limit_bytes=64 * 1024 * 1024),
        cost_estimate=pl.CostEstimate(flops=1_200_000_000, bytes_accessed=4_500_000, transcendentals=700_000),
        name="item_grad",
    )(length, me, *loaded)


def sum_rows(row_refs, bucket):
    total = jnp.zeros((bucket.shape[0], row_refs[0].shape[1]), f32)
    for rows_ref in row_refs:
        ids = rows_ref[CAP:, :CAP].astype(f32)
        slot_id = ids[0:1] * ID_BASE + ids[1:2]
        slot_id = jnp.where(ids[2:3] > 0.5, slot_id, -1.0).astype(jnp.int32)
        chosen = jnp.where(bucket == slot_id, 1.0, 0.0).astype(bf16)
        total = total + dot(chosen, rows_ref[:CAP, :])
    return total


def hot_kernel(cores, first, base_ref, rows_ref, out_ref):
    z_size = out_ref.shape[0]
    place = lax.broadcasted_iota(jnp.int32, (z_size * HOT_DEV, CAP), 0)
    z = first - place // HOT_DEV
    z = jnp.where(z < 0, z + z_size, z)
    bucket = z * (HOT_DEV * cores) + place % HOT_DEV + base_ref[0]
    out_ref[...] = sum_rows([rows_ref.at[i] for i in range(rows_ref.shape[0])], bucket).reshape(out_ref.shape).astype(bf16)


def hot_call(z_size, cores, first, base, rows):
    whole = pl.BlockSpec(memory_space=pltpu.VMEM)
    return pl.pallas_call(
        functools.partial(hot_kernel, cores, first),
        in_specs=[pl.BlockSpec(memory_space=pltpu.SMEM), whole],
        out_specs=whole,
        out_shape=jax.ShapeDtypeStruct((z_size, HOT_DEV, rows.shape[2]), bf16),
        compiler_params=pltpu.CompilerParams(vmem_limit_bytes=16 * 1024 * 1024),
        cost_estimate=pl.CostEstimate(flops=80_000_000, bytes_accessed=800_000, transcendentals=0),
        name="hot_sum",
    )(base, rows)


def cold_kernel(*refs):
    refs[-1][...] = sum_rows(refs[:-1], lax.broadcasted_iota(jnp.int32, (COLD_DEV, CAP), 0))


def cold_call(rows):
    whole = pl.BlockSpec(memory_space=pltpu.VMEM)
    return pl.pallas_call(
        cold_kernel,
        in_specs=[whole] * len(rows),
        out_specs=whole,
        out_shape=jax.ShapeDtypeStruct((COLD_DEV, rows[0].shape[1]), f32),
        compiler_params=pltpu.CompilerParams(vmem_limit_bytes=16 * 1024 * 1024),
        cost_estimate=pl.CostEstimate(flops=40_000_000, bytes_accessed=600_000, transcendentals=0),
        name="cold_sum",
    )(*rows)


def spread_kernel(parts_ref, out_ref):
    total = parts_ref[0].astype(f32)
    for i in range(1, parts_ref.shape[0]):
        total = total + parts_ref[i].astype(f32)
    for i in range(out_ref.shape[0]):
        out_ref[i] = total


def spread_call(owners, parts):
    whole = pl.BlockSpec(memory_space=pltpu.VMEM)
    return pl.pallas_call(
        spread_kernel,
        in_specs=[whole],
        out_specs=whole,
        out_shape=jax.ShapeDtypeStruct((owners,) + parts.shape[1:], f32),
        compiler_params=pltpu.CompilerParams(vmem_limit_bytes=16 * 1024 * 1024),
        cost_estimate=pl.CostEstimate(flops=70_000, bytes_accessed=160_000, transcendentals=0),
        name="spread",
    )(parts)


def shards(embeddings, lengths, cotangent, w_proj, w_out, routes, hot_ids, cold_ids):
    owners = lax.axis_size("table")
    z_size, cores = lax.axis_size("z"), lax.axis_size("core")
    seq, width = embeddings.shape[1:]
    me = lax.axis_index("table").reshape(1).astype(jnp.int32)
    own_rows, *sent, hot_rows = item_call(
        owners, lax.axis_size("y") * cores, lengths, me, embeddings.reshape(seq, width), cotangent.reshape(seq, width), w_proj, w_out,
        routes.reshape(1, seq), hot_ids, cold_ids,
    )
    gathered = lax.all_to_all(hot_rows, ("y", "core", "table"), 0, 0)
    base = lax.axis_index("y") * (z_size * cores * HOT_DEV) + lax.axis_index("core") * HOT_DEV
    first = z_size * 5 // 8
    order = [(first - i) % z_size for i in range(z_size)]
    partial = hot_call(z_size, cores, first, base.reshape(1).astype(jnp.int32), gathered)
    partial, sent = lax.optimization_barrier((partial, sent))
    parts = lax.all_to_all(partial, "z", 0, 0, axis_index_groups=[order])
    received = [
        lax.ppermute(rows, "table", [(i, (i + step) % owners) for i in range(owners)])
        for step, rows in enumerate(sent, start=1)
    ]
    cold_grad = cold_call([*received, own_rows])
    last = [(owners - 1 + i) % owners for i in range(owners)]
    copies = lax.all_to_all(spread_call(owners, parts), "table", 0, 0, axis_index_groups=[last])
    hot_grad = jnp.transpose(copies, (1, 0, 2)).reshape(HOT_DEV, width)
    return (hot_grad, cold_grad)


def solution(mesh):
    dp, table = mesh.devices.shape
    cores, y_size = 2, 4
    fine = Mesh(mesh.devices.reshape(y_size, dp // (y_size * cores), cores, table), ("y", "z", "core", "table"))
    every = ("y", "z", "core", "table")
    return jax.shard_map(
        shards,
        mesh=fine,
        in_specs=(
            P(every, None, None),
            P(every),
            P(every, None, None),
            P(),
            P(),
            P(every, None, None),
            P(every, None),
            P(every, None),
        ),
        out_specs=(P(("y", "z", "core"), None), P(every, None)),
        check_vma=False,
    )
```
